32 devices in a mesh: row: 4 (over y, core), col: 8 (over z, x).
Axes of the slice: x: 2, y: 2, z: 4, core: 2. Of those that a mesh axis runs over, the one named last changes fastest.
Arguments:
- amplitudes: bfloat16 [2048, 2048], P('row', 'col'), may hold values from -6 to 6
- integrals: bfloat16 [400, 400], replicated, may hold values from -0.3125 to 0.3125
- targets: int32 [110, 2048], replicated, may hold values from 0 to 2047
- pairs: int32 [110, 2048], replicated, may hold values from 0 to 399, as said below
- parity: int32 [110, 2048], replicated, may hold values 0 or 1
- alpha_window: int32 [768], P('row'), may hold values from 0 to 2047
- beta_window: int32 [768], P('col'), may hold values from 0 to 2047
Outputs:
- sigma: float32 [2048, 2048], P('row', 'col')
The draws below stay inside these ranges and needn't reach their ends.
Inputs may be any that keep to these rules, and one draw needn't show every extreme that they name: Each string has 110 distinct pairs: for each of its 10 occupied orbitals l, the pairs k * 20 + l with k unoccupied or k = l.
All inputs are finite; a program needn't handle non-finite values.
Results may differ from the reference program's by a relative error of at most 0.0029.
Values may be sent and summed in bfloat16 or wider, within the bound.
A program may use at most 128 MiB of HBM per device.

```python
import math
import jax
import jax.numpy as jnp
import numpy as np
from jax import lax

ORB = 20
NEX = 110
S = 2048
WA = 768
WB = 768


def one_order(subkey):
    return jax.random.permutation(subkey, ORB)


def draw_pairs(key, part):
    keys = jax.random.split(jax.random.fold_in(key, 17), S)
    orders = jax.vmap(one_order)(keys).astype(jnp.int32)
    half = ORB // 2
    occupied = orders[:, :half]
    vacant = orders[:, half:]
    spread = jnp.broadcast_to(vacant[:, None, :], (S, half, ORB - half))
    creators = jnp.concatenate([spread, occupied[:, :, None]], axis=2)
    removers = jnp.broadcast_to(occupied[:, :, None], creators.shape)
    pair_ids = creators * ORB + removers
    return pair_ids.reshape(S, half * (ORB - half + 1)).T.astype(jnp.int32)


def with_ends(values, rng, low, high):
    shape = values.shape
    spot = [jax.random.randint(jax.random.fold_in(rng, axis), (), 0, shape[axis]) for axis in range(len(shape))]
    values = values.at[tuple(spot)].set(low)
    longest = shape.index(max(shape))
    spot[longest] = (spot[longest] + 1) % shape[longest]
    return values.at[tuple(spot)].set(high)


def level_of(stream_key, shape, cuts, smallest, top_value):
    loudness = 1.0
    for dim, shards_of in cuts:
        steps = jax.random.uniform(jax.random.fold_in(jax.random.fold_in(stream_key, 6), dim), (shards_of,), jnp.float32, smallest / len(cuts), top_value / len(cuts))
        loudness = loudness * jnp.repeat(jnp.exp(steps), shape[dim] // shards_of).reshape((-1,) + (1,) * (len(shape) - 1 - dim))
    return loudness


def rank_bounds(number_of, skew):
    loads = [(1 << 20) // math.isqrt(grade ** skew) + 1 for grade in range(1, number_of + 1)]
    scale = 1 + sum(loads) // (1 << 30)
    return np.cumsum(np.array([max(1, weight // scale) for weight in loads]))


def ranked(key, dims, number_of, slope):
    grid = rank_bounds(number_of, slope)
    pick = jax.random.randint(jax.random.fold_in(key, 1), dims, 0, int(grid[number_of - 1]))
    grade = jnp.searchsorted(jnp.asarray(grid, jnp.int32), pick, side="right")
    return jax.random.permutation(jax.random.fold_in(key, 2), number_of)[grade].astype(jnp.int32)


def bell_draw(stream_key, shape, scale, reach, cuts=(), held_as=jnp.bfloat16):
    gain = level_of(stream_key, shape, cuts, -0.22, 0.18) if cuts else 1.0
    drawn = jax.random.normal(stream_key, shape, jnp.float32) * scale * gain
    return jnp.minimum(jnp.maximum(drawn, -reach), reach).astype(held_as)


def setup_inputs(seed: int = 0) -> dict:
    key_list = jax.random.split(jax.random.key(seed), 8)
    amplitudes = bell_draw(key_list[0], (S, S), 1.0, 6.0, ((0, 4), (1, 8)))
    integrals = bell_draw(key_list[1], (ORB * ORB, ORB * ORB), (ORB * ORB) ** -0.5, 0.3125)
    targets = with_ends(ranked(key_list[2], (NEX, S), S, 1), jax.random.fold_in(key_list[2], 3), 0, S - 1).astype(jnp.int32)
    pairs = draw_pairs(jax.random.fold_in(key_list[7], 71), 0)
    parity = with_ends((jax.random.randint(key_list[4], (NEX, S), 0, 2) < 1).astype(jnp.int32), jax.random.fold_in(key_list[4], 1), 0, 1)
    alpha_window = with_ends(jax.random.randint(key_list[5], (WA,), 0, S), jax.random.fold_in(key_list[5], 1), 0, S - 1).astype(jnp.int32)
    beta_window = with_ends(jax.random.randint(key_list[6], (WB,), 0, S), jax.random.fold_in(key_list[6], 1), 0, S - 1).astype(jnp.int32)
    return dict(amplitudes=amplitudes, integrals=integrals, targets=targets, pairs=pairs, parity=parity, alpha_window=alpha_window, beta_window=beta_window)


def pick_rows(matrix, indices):
    return jnp.take(matrix, indices, axis=0)


def side_terms(columns, targets, pairs, parity, window, integrals):
    target_ids = jnp.take(targets, window, axis=1).T.astype(jnp.int32)
    pair_ids = jnp.take(pairs, window, axis=1).T.astype(jnp.int32)
    sign_values = 1.0 - 2.0 * jnp.take(parity, window, axis=1).T.astype(jnp.float32)
    swap_ids = ((pair_ids % ORB) * ORB + pair_ids // ORB).astype(jnp.int32)
    blocks = target_ids.shape[0] // 16
    width = columns.shape[1]

    def shaped(array):
        return array.reshape((blocks, 16) + array.shape[1:])

    def one_block(partial_value, inputs):
        block_targets, block_pairs, block_swaps, block_signs = inputs
        rows = jnp.take(columns, block_targets, axis=0).astype(jnp.float32)
        weighted = jnp.take(integrals, block_pairs, axis=0).astype(jnp.float32) * block_signs[..., None]
        transformed = jnp.einsum("wen,wel->wnl", weighted, rows).astype(jnp.bfloat16)
        picked = jax.vmap(pick_rows)(transformed, block_swaps).astype(jnp.float32) * block_signs[..., None]
        partial_value = partial_value.at[block_targets.reshape(-1)].add(picked.reshape(-1, width))
        return partial_value, None

    start = jnp.zeros((columns.shape[0], width), jnp.float32)
    partial_value, unused = lax.scan(one_block, start, (shaped(target_ids), shaped(pair_ids), shaped(swap_ids), shaped(sign_values)))
    return partial_value


def reference(amplitudes, integrals, targets, pairs, parity, alpha_window, beta_window):
    alpha_part = side_terms(amplitudes, targets, pairs, parity, alpha_window, integrals)
    beta_part = side_terms(amplitudes.T, targets, pairs, parity, beta_window, integrals)
    return alpha_part + beta_part.T
```

```python
import jax
import jax.numpy as jnp
from jax import lax
from jax.experimental import pallas as pl
from jax.experimental.pallas import tpu as pltpu
from jax.sharding import PartitionSpec as P

ORB = 20
GROUP = 16
EROW = 112
ELANE = 128


def hamiltonian_kernel(t_flat, p_row, s_row, cols, integrals_t, out, xs):
    step = pl.program_id(0)
    strings, width = out.shape
    norb2 = integrals_t.shape[0]

    rows_p = lax.broadcasted_iota(jnp.int32, (norb2, GROUP * ELANE), 0)
    pick = jnp.where(rows_p == p_row[0], s_row[0], 0.0).astype(jnp.bfloat16)
    a_t = jnp.dot(integrals_t[...], pick, preferred_element_type=jnp.float32).astype(jnp.bfloat16)
    lanes_n = lax.broadcasted_iota(jnp.int32, (EROW, norb2), 1)
    lanes_t = lax.broadcasted_iota(jnp.int32, (ELANE, width), 1)
    for i in range(GROUP):
        q_col = cols[0, 0, :EROW, i : i + 1]
        sign_col = cols[0, 1, :EROW, i : i + 1].astype(jnp.float32)
        t_col = cols[0, 2, :, i : i + 1]
        select = jnp.where(lanes_n == q_col, sign_col, 0.0).astype(jnp.bfloat16)
        g = jnp.dot(
            select, a_t[:, i * ELANE : (i + 1) * ELANE], preferred_element_type=jnp.float32
        ).astype(jnp.bfloat16)
        spread = jnp.where(lanes_t == t_col, 1.0, 0.0).astype(jnp.bfloat16)
        xs[i * EROW : (i + 1) * EROW, :] = jnp.dot(
            g, spread, preferred_element_type=jnp.float32
        ).astype(jnp.bfloat16)

    tile = 256
    t_all = t_flat[0]
    rows_j = lax.broadcasted_iota(jnp.int32, (tile, GROUP * EROW), 0).astype(jnp.bfloat16)

    @pl.when(step == 0)
    def _():
        out[...] = jnp.zeros_like(out)

    def one_tile(m, carry):
        local = jnp.clip(t_all - m * tile, -1, tile).astype(jnp.bfloat16)
        hot = jnp.where(rows_j == local, jnp.bfloat16(1.0), jnp.bfloat16(0.0))
        where = pl.ds(pl.multiple_of(m * tile, tile), tile)
        out[where, :] += jnp.dot(hot, xs[...], preferred_element_type=jnp.float32)
        return carry

    lax.fori_loop(0, strings // tile, one_tile, 0)


def same_spin_matrix(t, p, sign, offset, integrals_t, strings, width):
    windows, nex = t.shape
    groups = windows // GROUP
    q = p % ORB * ORB + p // ORB

    def padded(array, size, fill):
        return jnp.pad(array, ((0, 0), (0, size - nex)), constant_values=fill)

    t_flat = padded(t, EROW, -1).reshape(groups, 1, GROUP * EROW)
    p_row = padded(p, ELANE, -1).reshape(groups, 1, GROUP * ELANE)
    s_row = padded(sign, ELANE, 0).astype(jnp.float32).reshape(groups, 1, GROUP * ELANE)
    cols = jnp.stack([padded(q, ELANE, -1), padded(sign, ELANE, 0), padded(t - offset, ELANE, -1)])
    cols = cols.reshape(3, groups, GROUP, ELANE).transpose(1, 0, 3, 2)
    norb2 = integrals_t.shape[0]
    flops = 2 * strings * width * windows * EROW
    return pl.pallas_call(
        hamiltonian_kernel,
        grid=(groups,),
        in_specs=[
            pl.BlockSpec((1, 1, GROUP * EROW), lambda g: (g, 0, 0)),
            pl.BlockSpec((1, 1, GROUP * ELANE), lambda g: (g, 0, 0)),
            pl.BlockSpec((1, 1, GROUP * ELANE), lambda g: (g, 0, 0)),
            pl.BlockSpec((1, 3, ELANE, GROUP), lambda g: (g, 0, 0, 0)),
            pl.BlockSpec((norb2, norb2), lambda g: (0, 0)),
        ],
        out_specs=pl.BlockSpec((strings, width), lambda g: (0, 0)),
        out_shape=jax.ShapeDtypeStruct((strings, width), jnp.float32),
        scratch_shapes=[
            pltpu.VMEM((GROUP * EROW, width), jnp.bfloat16),
        ],
        compiler_params=pltpu.CompilerParams(vmem_limit_bytes=50 * 1024 * 1024),
        cost_estimate=pl.CostEstimate(
            flops=flops, bytes_accessed=strings * width * 4, transcendentals=0
        ),
    )(t_flat, p_row, s_row, cols, integrals_t)


def window_lists(targets, pairs, parity, window):
    nex, strings = targets.shape
    code = targets + pairs * 4096
    parts = jnp.concatenate(
        [code % 256, code // 256 % 256, code // 65536 + parity * 64], axis=0
    ).astype(jnp.bfloat16)
    hot = (window[:, None] == lax.broadcasted_iota(jnp.int32, (1, strings), 1)).astype(jnp.bfloat16)
    got = lax.dot_general(
        hot, parts, (((1,), (1,)), ((), ())), preferred_element_type=jnp.float32
    ).astype(jnp.int32)
    low, middle, high = got[:, :nex], got[:, nex : 2 * nex], got[:, 2 * nex :]
    code = low + middle * 256 + high % 64 * 65536
    return code % 4096, code // 4096, 1 - 2 * (high // 64)


def on_device(amplitudes, integrals, targets, pairs, parity, alpha_window, beta_window):
    rows, columns = amplitudes.shape
    strings = targets.shape[1]
    window = jnp.concatenate([alpha_window, beta_window])
    t, p, sign = window_lists(targets, pairs, parity, window)
    na = alpha_window.shape[0]
    alpha_columns = lax.all_gather(amplitudes, "row", axis=0, tiled=True)
    beta_columns = lax.all_gather(amplitudes, "col", axis=1, tiled=True)
    integrals_t = integrals.T
    beta_partial = same_spin_matrix(
        t[na:], p[na:], sign[na:], lax.axis_index("row") * rows, integrals_t, strings, rows
    )
    alpha_partial = same_spin_matrix(
        t[:na], p[:na], sign[:na], lax.axis_index("col") * columns, integrals_t, strings, columns
    )
    beta_own = lax.psum_scatter(beta_partial, "col", scatter_dimension=0, tiled=True)
    beta_all = lax.all_gather(beta_own.astype(jnp.bfloat16), "row", axis=1, tiled=True)
    alpha_own = lax.psum_scatter(alpha_partial, "row", scatter_dimension=0, tiled=True)
    alpha_all = lax.all_gather(alpha_own.astype(jnp.bfloat16), "col", axis=1, tiled=True)
    beta_part = lax.dot_general(
        beta_columns, beta_all, (((1,), (1,)), ((), ())), preferred_element_type=jnp.float32
    )
    alpha_part = jnp.dot(alpha_all, alpha_columns, preferred_element_type=jnp.float32)
    return alpha_part + beta_part


def solution(mesh):
    in_specs = (P("row", "col"), P(), P(), P(), P(), P("row"), P("col"))
    out_specs = P("row", "col")
    return jax.shard_map(
        on_device, mesh=mesh, in_specs=in_specs, out_specs=out_specs, check_vma=False
    )
```

```python
import jax
import jax.numpy as jnp
from jax import lax
from jax.experimental import pallas as pl
from jax.experimental.pallas import tpu as pltpu
from jax.sharding import PartitionSpec as P

ORB = 20
GROUP = 16
EROW = 112
ELANE = 128


def hamiltonian_kernel(t_flat, p_row, s_row, cols, integrals_t, out, xs):
    step = pl.program_id(0)
    strings, width = out.shape
    norb2 = integrals_t.shape[0]

    rows_p = lax.broadcasted_iota(jnp.int32, (norb2, GROUP * ELANE), 0)
    pick = jnp.where(rows_p == p_row[0], s_row[0], 0.0).astype(jnp.bfloat16)
    a_t = jnp.dot(integrals_t[...], pick, preferred_element_type=jnp.float32).astype(jnp.bfloat16)
    lanes_n = lax.broadcasted_iota(jnp.int32, (EROW, norb2), 1)
    lanes_t = lax.broadcasted_iota(jnp.int32, (ELANE, width), 1)
    gs = []
    for i in range(GROUP):
        q_col = cols[0, 0, :EROW, i : i + 1]
        sign_col = cols[0, 1, :EROW, i : i + 1].astype(jnp.float32)
        select = jnp.where(lanes_n == q_col, sign_col, 0.0).astype(jnp.bfloat16)
        gs.append(
            jnp.dot(
                select, a_t[:, i * ELANE : (i + 1) * ELANE], preferred_element_type=jnp.float32
            ).astype(jnp.bfloat16)
        )
    for i in range(GROUP):
        t_col = cols[0, 2, :, i : i + 1]
        spread = jnp.where(lanes_t == t_col, 1.0, 0.0).astype(jnp.bfloat16)
        xs[i * EROW : (i + 1) * EROW, :] = jnp.dot(
            gs[i], spread, preferred_element_type=jnp.float32
        ).astype(jnp.bfloat16)

    tile = 256
    t_all = t_flat[0]
    rows_j = lax.broadcasted_iota(jnp.int32, (tile, GROUP * EROW), 0).astype(jnp.bfloat16)

    @pl.when(step == 0)
    def _():
        out[...] = jnp.zeros_like(out)

    def one_tile(m, carry):
        local = jnp.clip(t_all - m * tile, -1, tile).astype(jnp.bfloat16)
        hot = jnp.where(rows_j == local, jnp.bfloat16(1.0), jnp.bfloat16(0.0))
        where = pl.ds(pl.multiple_of(m * tile, tile), tile)
        out[where, :] += jnp.dot(hot, xs[...], preferred_element_type=jnp.float32)
        return carry

    lax.fori_loop(0, strings // tile, one_tile, 0)


def same_spin_matrix(t, p, sign, offset, integrals_t, strings, width):
    windows, nex = t.shape
    groups = windows // GROUP
    q = p % ORB * ORB + p // ORB

    def padded(array, size, fill):
        return jnp.pad(array, ((0, 0), (0, size - nex)), constant_values=fill)

    t_flat = padded(t, EROW, -1).reshape(groups, 1, GROUP * EROW)
    p_row = padded(p, ELANE, -1).reshape(groups, 1, GROUP * ELANE)
    s_row = padded(sign, ELANE, 0).astype(jnp.float32).reshape(groups, 1, GROUP * ELANE)
    cols = jnp.stack([padded(q, ELANE, -1), padded(sign, ELANE, 0), padded(t - offset, ELANE, -1)])
    cols = cols.reshape(3, groups, GROUP, ELANE).transpose(1, 0, 3, 2)
    norb2 = integrals_t.shape[0]
    flops = 2 * strings * width * windows * EROW
    return pl.pallas_call(
        hamiltonian_kernel,
        grid=(groups,),
        in_specs=[
            pl.BlockSpec((1, 1, GROUP * EROW), lambda g: (g, 0, 0)),
            pl.BlockSpec((1, 1, GROUP * ELANE), lambda g: (g, 0, 0)),
            pl.BlockSpec((1, 1, GROUP * ELANE), lambda g: (g, 0, 0)),
            pl.BlockSpec((1, 3, ELANE, GROUP), lambda g: (g, 0, 0, 0)),
            pl.BlockSpec((norb2, norb2), lambda g: (0, 0)),
        ],
        out_specs=pl.BlockSpec((strings, width), lambda g: (0, 0)),
        out_shape=jax.ShapeDtypeStruct((strings, width), jnp.float32),
        scratch_shapes=[
            pltpu.VMEM((GROUP * EROW, width), jnp.bfloat16),
        ],
        compiler_params=pltpu.CompilerParams(vmem_limit_bytes=50 * 1024 * 1024),
        cost_estimate=pl.CostEstimate(
            flops=flops, bytes_accessed=strings * width * 4, transcendentals=0
        ),
    )(t_flat, p_row, s_row, cols, integrals_t)


def window_lists(targets, pairs, parity, window):
    nex, strings = targets.shape
    code = targets + pairs * 4096
    parts = jnp.concatenate(
        [code % 256, code // 256 % 256, code // 65536 + parity * 64], axis=0
    ).astype(jnp.bfloat16)
    hot = (window[:, None] == lax.broadcasted_iota(jnp.int32, (1, strings), 1)).astype(jnp.bfloat16)
    got = lax.dot_general(
        hot, parts, (((1,), (1,)), ((), ())), preferred_element_type=jnp.float32
    ).astype(jnp.int32)
    low, middle, high = got[:, :nex], got[:, nex : 2 * nex], got[:, 2 * nex :]
    code = low + middle * 256 + high % 64 * 65536
    return code % 4096, code // 4096, 1 - 2 * (high // 64)


def shifted(block, axis_name):
    n = lax.axis_size(axis_name)
    blocks = [block]
    for k in range(1, n):
        blocks.append(lax.ppermute(block, axis_name, [((i + k) % n, i) for i in range(n)]))
    return blocks


def in_order(blocks, axis_name, dim):
    n, size = len(blocks), blocks[0].shape[dim]
    twice = jnp.concatenate(blocks + blocks, axis=dim)
    start = (n - lax.axis_index(axis_name)) * size
    return lax.dynamic_slice_in_dim(twice, start, n * size, axis=dim)


def on_device(amplitudes, integrals, targets, pairs, parity, alpha_window, beta_window):
    rows, columns = amplitudes.shape
    strings = targets.shape[1]
    window = jnp.concatenate([alpha_window, beta_window])
    t, p, sign = window_lists(targets, pairs, parity, window)
    na = alpha_window.shape[0]
    row, col = lax.axis_index("row"), lax.axis_index("col")
    n_row, n_col = lax.axis_size("row"), lax.axis_size("col")
    row_blocks = shifted(amplitudes, "row")
    col_blocks = shifted(amplitudes, "col")
    integrals_t = integrals.T
    beta_partial = same_spin_matrix(
        t[na:], p[na:], sign[na:], row * rows, integrals_t, strings, rows
    )
    beta_own = lax.psum_scatter(beta_partial, "col", scatter_dimension=0, tiled=True)
    alpha_partial = same_spin_matrix(
        t[:na], p[:na], sign[:na], col * columns, integrals_t, strings, columns
    )
    alpha_own = lax.psum_scatter(alpha_partial, "row", scatter_dimension=0, tiled=True)
    alpha_columns = in_order(row_blocks, "row", 0)
    beta_columns = in_order(col_blocks, "col", 1)
    total = jnp.zeros((rows, columns), jnp.float32)
    for k, block in enumerate(shifted(beta_own.astype(jnp.bfloat16), "row")):
        start = (row + k) % n_row * rows
        part = lax.dynamic_slice_in_dim(beta_columns, start, rows, axis=1)
        total += lax.dot_general(
            part, block, (((1,), (1,)), ((), ())), preferred_element_type=jnp.float32
        )
    for k, block in enumerate(shifted(alpha_own.astype(jnp.bfloat16), "col")):
        start = (col + k) % n_col * columns
        part = lax.dynamic_slice_in_dim(alpha_columns, start, columns, axis=0)
        total += jnp.dot(block, part, preferred_element_type=jnp.float32)
    return total


def solution(mesh):
    in_specs = (P("row", "col"), P(), P(), P(), P(), P("row"), P("col"))
    out_specs = P("row", "col")
    return jax.shard_map(
        on_device, mesh=mesh, in_specs=in_specs, out_specs=out_specs, check_vma=False
    )
```
